128 devices in a mesh: row: 4 (over x_hi, core), col: 32 (over z, y, x_lo).
Axes of the slice: x: 4 (x_hi: 2, x_lo: 2; x = x_hi * 2 + x_lo), y: 4, z: 4, core: 2. Of those that a mesh axis runs over, the one named last changes fastest.
Arguments:
- t_store: bfloat16 [8192, 1024], P(('row', 'col')), may hold values from -24 to 24
- w_panels: bfloat16 [1024, 65536], P('row', 'col'), may hold values from -0.1875 to 0.1875
- block_place: int32 [1024], replicated, may hold values from 0 to 1023, as said below
- occ_energy: float32 [64], replicated, may hold values from -3 to -0.5
- vir_energy: float32 [1024], replicated, may hold values from 0.3 to 4
- vir_order: int32 [1024], replicated, may hold values from 0 to 1023, each once
Outputs:
- updated: float32 [8192, 65536], P('row', 'col')
The draws below stay inside these ranges and needn't reach their ends.
Inputs may be any that keep to these rules, and one draw needn't show every extreme that they name: block_place is a permutation of the blocks in which slot s and block block_place[s] lie in the same group of 256 consecutive indices.
All inputs are finite; a program needn't handle non-finite values.
Results may differ from the reference program's by a relative error of at most 0.0003.
Values may be sent and summed in bfloat16 or wider, within the bound.
No kernel may reach another device: no remote copies, remote signals or barrier semaphores. Data moves between devices by JAX's collectives and lax.ppermute only.
A program may use at most 128 MiB of HBM per device.

```python
import jax
import jax.numpy as jnp
from jax import lax

NOCC = 64
NVIR = 1024
ROW_DEV = 2048
BLK = 8
K = 1024
ROWS = 8192
ORDER = 65536
BLOCKS = 1024


def draw_block_place(key, part):
    key = jax.random.fold_in(key, 11)
    groups = ROWS // ROW_DEV
    per_group = ROW_DEV // BLK
    keys = jax.random.split(key, groups)
    orders = jax.vmap(lambda single: jax.random.permutation(single, per_group))(keys)
    shifted = orders + (jnp.arange(groups) * per_group)[:, None]
    return shifted.reshape(-1).astype(jnp.int32)


def block_scale(own_key, shape, cuts, smallest, largest):
    def one(dim, parts):
        heights = jax.random.uniform(jax.random.fold_in(jax.random.fold_in(own_key, 6), dim), (parts,), jnp.float32, smallest / len(cuts), largest / len(cuts))
        return jnp.repeat(jnp.exp(heights), shape[dim] // parts).reshape((-1,) + (1,) * (len(shape) - dim - 1))

    gain = one(*cuts[0])
    for cut in cuts[1:]:
        gain = gain * one(*cut)
    return gain


def normal_values(key, extent, width, reach, cuts=(), kind=jnp.bfloat16):
    values = width * jax.random.normal(key, extent, jnp.float32)
    if cuts:
        values = values * block_scale(key, extent, cuts, -0.22, 0.18)
    return jnp.clip(values, -reach, reach).astype(kind)


def setup_inputs(seed: int = 0) -> dict:
    seeds = jax.random.split(jax.random.key(seed), 7)
    return {
        "t_store": normal_values(seeds[0], (ROWS, K), 4.0, 24.0, ((0, 128),)),
        "w_panels": normal_values(seeds[1], (K, ORDER), K ** -0.5, 0.1875, ((0, 4), (1, 32))),
        "block_place": draw_block_place(jax.random.fold_in(seeds[6], 71), 0),
        "occ_energy": jnp.clip(jax.random.uniform(seeds[3], (NOCC,), jnp.float32, -3.0, -0.5), -3.0, -0.5),
        "vir_energy": jnp.clip(jax.random.uniform(seeds[4], (NVIR,), jnp.float32, 0.3, 4.0), 0.3, 4.0),
        "vir_order": jax.random.permutation(seeds[5], NVIR).astype(jnp.int32),
    }


def reference(t_store, w_panels, block_place, occ_energy, vir_energy, vir_order):
    blocks = t_store.reshape(BLOCKS, BLK, K)
    placed = jnp.zeros_like(blocks).at[block_place].set(blocks).reshape(ROWS, K).astype(jnp.float32)
    vir_eff = vir_energy[vir_order]
    occ_rep = jnp.repeat(occ_energy, NVIR)
    vir_rep = jnp.tile(vir_eff, NOCC)
    row_occ = occ_rep[:ROWS]
    row_vir = vir_rep[:ROWS]

    def column_block(column_step, result):
        offset = (column_step * NVIR).astype(jnp.int32)
        weights = lax.dynamic_slice_in_dim(w_panels, offset, NVIR, 1).astype(jnp.float32)
        col_occ = lax.dynamic_slice_in_dim(occ_rep, offset, NVIR, 0)
        col_vir = lax.dynamic_slice_in_dim(vir_rep, offset, NVIR, 0)
        cycle_part = jnp.dot(placed, weights, precision=lax.Precision.HIGHEST)
        denominator = (row_occ[:, None] + col_occ[None, :]) - (row_vir[:, None] + col_vir[None, :])
        return lax.dynamic_update_slice_in_dim(result, cycle_part / denominator, offset, 1)

    return lax.fori_loop(0, NOCC, column_block, jnp.zeros((ROWS, ORDER), jnp.float32))
```

```python
import functools

import jax
import jax.numpy as jnp
import numpy as np
from jax import lax
from jax.experimental import pallas as pl
from jax.experimental.pallas import tpu as pltpu
from jax.sharding import PartitionSpec as P

NVIR = 1024
BLK = 8
RING = 4
PIECE = 256
TILE = 256


def move(target):
    pairs = []
    for src in range(128):
        row, col = divmod(src, 32)
        place = (row // 2) * 2 + col % 2, col // 2 % RING, col // 8, row % 2
        x, y, z, core = target(*place)
        x, y, z = x % RING, y % RING, z % RING
        pairs.append((src, (x // 2 * 2 + core) * 32 + z * 8 + y * 2 + x % 2))
    return pairs


def along_first(step):
    return move(lambda x, y, z, core: (x, y + step, z, core) if core == 0 else (x, y, z + step, core))


def along_second(step):
    return move(lambda x, y, z, core: (x, y, z + step, core) if core == 0 else (x, y + step, z, core))


ACROSS_LO = move(lambda x, y, z, core: (x ^ 1, y, z, core))
ACROSS_HI = move(lambda x, y, z, core: (x + 2, y, z, core))
OTHER_CORE = move(lambda x, y, z, core: (x, y, z, 1 - core))


def send(value, pairs):
    return lax.ppermute(value, ("row", "col"), pairs)


def multiply(ids, parts, offset, *refs):
    n = len(ids)
    origin, block_place, row_term, col_term = refs[:4]
    pieces = refs[4 : 4 + n]
    panels = refs[4 + n : 4 + n + 4 * parts]
    out, stage, row_part, sem = refs[-4:]
    cols = panels[0].shape[1]
    grid_row = origin[32]

    def place(piece, i):
        slot = origin[ids[piece] * 4 + i // BLK] * BLK + i % BLK
        return block_place[slot] - grid_row * 256

    for piece in range(n):

        def fill(i, carry):
            at = pl.multiple_of(place(piece, i) * BLK, BLK)
            to = pl.multiple_of(piece * PIECE + i * BLK, BLK)
            row_part[pl.ds(to, BLK), :] = row_term[pl.ds(at, BLK), :]
            return carry

        lax.fori_loop(0, PIECE // BLK, fill, 0, unroll=8)
        rows = pl.ds(piece * PIECE, PIECE)
        for part in range(parts):

            def tile(i, carry):
                at = pl.ds(pl.multiple_of(i * TILE, TILE), TILE)
                to = pl.ds(pl.multiple_of(part * cols + i * TILE, TILE), TILE)
                total = None
                for k in range(4):
                    depth = pl.ds(pl.multiple_of((grid_row ^ k) * 256, 256), 256)
                    term = jnp.dot(
                        pieces[piece][:, depth],
                        panels[part * 4 + k][:, at],
                        preferred_element_type=jnp.float32,
                    )
                    total = term if total is None else total + term
                left = row_part[rows, :]
                denominator = jnp.concatenate([left] * (TILE // 128), axis=1) + col_term[:, to]
                inverse = pltpu.reciprocal(denominator, approx=True)
                inverse = inverse * (2.0 - denominator * inverse)
                stage[rows, to] = total * inverse
                return carry

            lax.fori_loop(0, cols // TILE, tile, 0, unroll=4)

        def put(i, carry):
            at = pl.multiple_of(piece * PIECE + i * BLK, BLK)
            to = pl.multiple_of(place(piece, i) * BLK, BLK)
            pltpu.make_async_copy(
                stage.at[pl.ds(at, BLK), :],
                out.at[pl.ds(to, BLK), pl.ds(offset, cols * parts)],
                sem,
            ).start()
            return carry

        lax.fori_loop(0, PIECE // BLK, put, 0, unroll=8)
    pltpu.make_async_copy(
        stage, out.at[pl.ds(0, n * PIECE), pl.ds(offset, cols * parts)], sem
    ).wait()


def contract(result, origin, block_place, row_term, col_term, pieces, panels, offset, shape):
    ids = tuple(pieces)
    parts = len(panels)
    cols = panels[0][0].shape[1] * parts
    operands = [origin, block_place, row_term, col_term[:, offset : offset + cols]]
    operands += list(pieces.values()) + [chunk for part in panels for chunk in part]
    vmem = pl.BlockSpec(memory_space=pltpu.VMEM)
    smem = pl.BlockSpec(memory_space=pltpu.SMEM)
    anywhere = pl.BlockSpec(memory_space=pl.ANY)
    specs = [smem, smem] + [vmem] * (len(operands) - 2)
    alias = {}
    if result is not None:
        alias = {len(operands): 0}
        operands.append(result)
        specs.append(anywhere)
    rows = len(ids) * PIECE
    return pl.pallas_call(
        functools.partial(multiply, ids, parts, offset),
        out_shape=jax.ShapeDtypeStruct(shape, jnp.float32),
        in_specs=specs,
        out_specs=anywhere,
        input_output_aliases=alias,
        scratch_shapes=[
            pltpu.VMEM((rows, cols), jnp.float32),
            pltpu.VMEM((rows, 128), jnp.float32),
            pltpu.SemaphoreType.DMA,
        ],
        compiler_params=pltpu.CompilerParams(vmem_limit_bytes=16 * 2**20),
        cost_estimate=pl.CostEstimate(
            flops=2 * rows * cols * 1024, bytes_accessed=rows * cols * 4, transcendentals=0
        ),
    )(*operands)


NEAR = (0, 3)
FAR = (1, 2)
PIECES = [(NEAR, 0), (FAR, 0), (NEAR, 3), (FAR, 1), (FAR, 3), (NEAR, 1), (NEAR, 2), (FAR, 2)]


def per_device(t_store, w_panels, block_place, occ_energy, vir_energy, vir_order):
    grid_row = lax.axis_index("row")
    grid_col = lax.axis_index("col")
    core = grid_row % 2
    col_dev = w_panels.shape[1]
    row_dev = 2048

    pair = jnp.concatenate([t_store, send(t_store, ACROSS_LO)])
    near = jnp.concatenate([pair, send(pair, along_first(1))])
    far = jnp.concatenate([send(pair, along_first(-1)), send(pair, along_first(2))])
    near_up = send(near, along_second(1))
    far_down = send(far, along_second(-1))
    far_up = send(far, along_second(1))
    near_down = send(near, along_second(-1))
    near_two = send(near_up, along_second(1))
    far_two = send(far_down, along_second(-1))

    half = col_dev // 2
    gate, gated = lax.optimization_barrier((pair, w_panels))
    own = [w_panels[:, :half], w_panels[:, half:]]
    beside = [send(part, OTHER_CORE) for part in own]
    across = [send(gated[:, :half], ACROSS_HI), send(gated[:, half:], ACROSS_HI)]
    aslant = [send(part, OTHER_CORE) for part in across]
    panels = [list(part) for part in zip(own, beside, across, aslant)]

    first = np.array([step for steps, _ in PIECES for step in steps for _ in range(2)], np.int32)
    second = np.array([step for steps, step in PIECES for _ in range(4)], np.int32)
    other = np.array([0, 1] * 16, np.int32)
    y, z, lo = grid_col // 2 % RING, grid_col // 8, grid_col % 2
    at_first = (jnp.where(core == 0, y, z) + first) % RING
    at_second = (jnp.where(core == 0, z, y) + second) % RING
    at_y = jnp.where(core == 0, at_first, at_second)
    at_z = jnp.where(core == 0, at_second, at_first)
    origin = grid_row * 32 + at_z * 8 + at_y * 2 + (lo ^ other)
    origin = jnp.concatenate([origin, grid_row[None]]).astype(jnp.int32)

    indices = jnp.arange(NVIR, dtype=jnp.int32)
    vir_eff = jnp.sum(
        jnp.where(vir_order[:, None] == indices[None, :], vir_energy[None, :], 0.0), axis=1
    )
    row_occ = lax.dynamic_slice_in_dim(occ_energy, grid_row * 2, 2, 0)
    col_occ = lax.dynamic_slice_in_dim(occ_energy, grid_col * 2, 2, 0)
    row_term = jnp.broadcast_to(
        (row_occ[:, None] - vir_eff[None, :]).reshape(row_dev, 1), (row_dev, 128)
    )
    col_term = (col_occ[:, None] - vir_eff[None, :]).reshape(1, col_dev)

    shape = (row_dev, col_dev)
    step = lambda result, pieces, part, offset: contract(
        result, origin, block_place, row_term, col_term, pieces, part, offset, shape
    )
    result = step(None, {0: near, 1: far, 2: near_up}, panels[:1], 0)
    result = step(result, {3: far_down, 4: far_up, 5: near_down}, panels[:1], 0)
    early = {0: near, 1: far, 2: near_up, 3: far_down, 4: far_up, 5: near_down}
    result = step(result, early, panels[1:], half)
    return step(result, {6: near_two, 7: far_two}, panels, 0)


def solution(mesh):
    in_specs = (P(("row", "col"), None), P("row", "col"), P(), P(), P(), P())
    out_specs = P("row", "col")
    return jax.shard_map(
        per_device, mesh=mesh, in_specs=in_specs, out_specs=out_specs, check_vma=False
    )
```

```python
import functools

import jax
import jax.numpy as jnp
import numpy as np
from jax import lax
from jax.experimental import pallas as pl
from jax.experimental.pallas import tpu as pltpu
from jax.sharding import PartitionSpec as P

NVIR = 1024
BLK = 8
RING = 4
PIECE = 256
TILE = 256


def move(target):
    pairs = []
    for src in range(128):
        row, col = divmod(src, 32)
        place = (row // 2) * 2 + col % 2, col // 2 % RING, col // 8, row % 2
        x, y, z, core = target(*place)
        x, y, z = x % RING, y % RING, z % RING
        pairs.append((src, (x // 2 * 2 + core) * 32 + z * 8 + y * 2 + x % 2))
    return pairs


def along_first(step):
    return move(lambda x, y, z, core: (x, y + step, z, core) if core == 0 else (x, y, z + step, core))


def along_second(step):
    return move(lambda x, y, z, core: (x, y, z + step, core) if core == 0 else (x, y + step, z, core))


ACROSS_LO = move(lambda x, y, z, core: (x ^ 1, y, z, core))
ACROSS_HI = move(lambda x, y, z, core: (x + 2, y, z, core))
OTHER_CORE = move(lambda x, y, z, core: (x, y, z, 1 - core))


def send(value, pairs):
    return lax.ppermute(value, ("row", "col"), pairs)


def after(value, *others):
    return lax.optimization_barrier((value, *others))[0]


def join_kernel(first, second, out):
    rows = first.shape[0]
    out[:rows, :] = first[...]
    out[rows:, :] = second[...]


def load_kernel(source, out, sem):
    copy = pltpu.make_async_copy(source, out, sem)
    copy.start()
    copy.wait()


def load(source):
    return pl.pallas_call(
        load_kernel,
        out_shape=jax.ShapeDtypeStruct(source.shape, source.dtype),
        in_specs=[pl.BlockSpec(memory_space=pl.ANY)],
        out_specs=pl.BlockSpec(memory_space=pltpu.VMEM),
        scratch_shapes=[pltpu.SemaphoreType.DMA],
        compiler_params=limits(1),
        cost_estimate=cost(0, 2**20),
    )(source)


def join(first, second):
    rows, cols = first.shape
    vmem = pl.BlockSpec(memory_space=pltpu.VMEM)
    return pl.pallas_call(
        join_kernel,
        out_shape=jax.ShapeDtypeStruct((2 * rows, cols), first.dtype),
        in_specs=[vmem, vmem],
        out_specs=vmem,
        compiler_params=limits(4),
        cost_estimate=cost(0, 8 * rows * cols),
    )(first, second)


def arrange(origin, block_place, row_term, row_part, places):
    grid_row = origin[32]

    def block(i, carry):
        place = block_place[origin[i // BLK] * BLK + i % BLK] - grid_row * 256
        places[i] = place
        at, to = pl.multiple_of(place * BLK, BLK), pl.multiple_of(i * BLK, BLK)
        row_part[pl.ds(to, BLK), :] = row_term[pl.ds(at, BLK), :]
        return carry

    lax.fori_loop(0, 256, block, 0, unroll=8)


def begin(pair, origin, *refs):
    first, second, own, beside = refs[:4]
    held, sums = refs[-2:]
    grid_row = origin[32]
    rows = pl.ds(pair * 2 * PIECE, 2 * PIECE)
    held[pl.ds(pair * 2 * PIECE, PIECE), :] = first[...]
    held[pl.ds((pair * 2 + 1) * PIECE, PIECE), :] = second[...]

    def tile(i, carry):
        at = pl.ds(pl.multiple_of(i * TILE, TILE), TILE)
        total = None
        for chunk, panel in enumerate((own, beside)):
            depth = pl.ds(pl.multiple_of((grid_row ^ chunk) * 256, 256), 256)
            left = jnp.concatenate([first[:, depth], second[:, depth]])
            term = jnp.dot(left, panel[:, at], preferred_element_type=jnp.float32)
            total = term if total is None else total + term
        sums[rows, at] = total
        return carry

    lax.fori_loop(0, sums.shape[1] // TILE, tile, 0, unroll=4)


def finish(origin, places, row_part, col_term, held, sums, across, aslant, out, stage, sem):
    cols = col_term.shape[1]
    tiles, blocks = cols // TILE, 2 * PIECE // BLK
    depths = [pl.ds(pl.multiple_of((origin[32] ^ chunk) * 256, 256), 256) for chunk in (2, 3)]

    def gone(slot):
        pltpu.make_async_copy(
            stage.at[slot], out.at[pl.ds(0, 2 * PIECE), :], sem.at[slot]
        ).wait()

    def work(pair, carry):
        slot = pair % 2
        rows = pl.ds(pl.multiple_of(pair * 2 * PIECE, 2 * PIECE), 2 * PIECE)

        @pl.when(pair > 1)
        def _():
            gone(slot)

        def tile(i, carry):
            at = pl.ds(pl.multiple_of(i * TILE, TILE), TILE)
            total = sums[rows, at]
            for depth, panel in zip(depths, (across, aslant)):
                total += jnp.dot(held[rows, depth], panel[:, at], preferred_element_type=jnp.float32)
            left = row_part[rows, :]
            denominator = jnp.concatenate([left] * (TILE // 128), axis=1) + col_term[:, at]
            inverse = pltpu.reciprocal(denominator, approx=True)
            inverse = inverse * (2.0 - denominator * inverse)
            stage[slot, :, at] = total * inverse
            return carry

        lax.fori_loop(0, tiles, tile, 0, unroll=8)

        def put(i, carry):
            at = pl.multiple_of(i * BLK, BLK)
            to = pl.multiple_of(places[pair * blocks + i] * BLK, BLK)
            pltpu.make_async_copy(
                stage.at[slot, pl.ds(at, BLK), :], out.at[pl.ds(to, BLK), :], sem.at[slot]
            ).start()
            return carry

        lax.fori_loop(0, blocks, put, 0, unroll=64)
        return carry

    lax.fori_loop(0, 4, work, 0)
    gone(0)
    gone(1)


VMEM = pl.BlockSpec(memory_space=pltpu.VMEM)
SMEM = pl.BlockSpec(memory_space=pltpu.SMEM)


def limits(mebibytes):
    return pltpu.CompilerParams(vmem_limit_bytes=mebibytes * 2**20)


def cost(flops, moved):
    return pl.CostEstimate(flops=flops, bytes_accessed=moved, transcendentals=0)


def arranged(origin, block_place, row_term):
    return pl.pallas_call(
        arrange,
        out_shape=[
            jax.ShapeDtypeStruct(row_term.shape, jnp.float32),
            jax.ShapeDtypeStruct((256,), jnp.int32),
        ],
        in_specs=[SMEM, SMEM, VMEM],
        out_specs=[VMEM, SMEM],
        compiler_params=limits(4),
        cost_estimate=cost(0, 2**21),
    )(origin, block_place, row_term)


def begun(pair, work, origin, pieces, own, beside, so_far, *awaited):
    cols, depth = own.shape[1], pieces[0].shape[1]
    shapes = [
        jax.ShapeDtypeStruct((8 * PIECE, depth), own.dtype),
        jax.ShapeDtypeStruct((8 * PIECE, cols), jnp.float32),
    ]
    operands = [origin, *pieces, own, beside, *so_far, *awaited]
    return pl.pallas_call(
        functools.partial(begin, pair),
        out_shape=shapes,
        in_specs=[SMEM]
        + [VMEM] * (len(operands) - 1 - len(awaited))
        + [pl.BlockSpec(memory_space=pl.ANY)] * len(awaited),
        out_specs=[VMEM, VMEM],
        input_output_aliases={5: 0, 6: 1} if so_far else {},
        compiler_params=limits(4),
        cost_estimate=cost(work, 2**21),
    )(*operands)


def finished(*operands):
    shape = operands[2].shape[0], operands[3].shape[1]
    return pl.pallas_call(
        finish,
        out_shape=jax.ShapeDtypeStruct(shape, jnp.float32),
        in_specs=[SMEM, SMEM] + [VMEM] * 6,
        out_specs=pl.BlockSpec(memory_space=pl.ANY),
        scratch_shapes=[
            pltpu.VMEM((2, 2 * PIECE, shape[1]), jnp.float32),
            pltpu.SemaphoreType.DMA((2,)),
        ],
        compiler_params=limits(12),
        cost_estimate=cost(1, 2**23),
    )(*operands)


NEAR = (0, 3)
FAR = (1, 2)
PIECES = [(NEAR, 0), (FAR, 0), (NEAR, 3), (FAR, 1), (FAR, 3), (NEAR, 1), (NEAR, 2), (FAR, 2)]


def per_device(t_store, w_panels, block_place, occ_energy, vir_energy, vir_order):
    grid_row = lax.axis_index("row")
    grid_col = lax.axis_index("col")
    core = grid_row % 2
    col_dev = w_panels.shape[1]
    row_dev = 2048

    first = np.array([step for steps, _ in PIECES for step in steps for _ in range(2)], np.int32)
    second = np.array([step for steps, step in PIECES for _ in range(4)], np.int32)
    other = np.array([0, 1] * 16, np.int32)
    y, z, lo = grid_col // 2 % RING, grid_col // 8, grid_col % 2
    at_first = (jnp.where(core == 0, y, z) + first) % RING
    at_second = (jnp.where(core == 0, z, y) + second) % RING
    at_y = jnp.where(core == 0, at_first, at_second)
    at_z = jnp.where(core == 0, at_second, at_first)
    origin = grid_row * 32 + at_z * 8 + at_y * 2 + (lo ^ other)
    origin = jnp.concatenate([origin, grid_row[None]]).astype(jnp.int32)

    indices = jnp.arange(NVIR, dtype=jnp.int32)
    vir_eff = jnp.sum(
        jnp.where(vir_order[:, None] == indices[None, :], vir_energy[None, :], 0.0), axis=1
    )
    row_occ = lax.dynamic_slice_in_dim(occ_energy, grid_row * 2, 2, 0)
    col_occ = lax.dynamic_slice_in_dim(occ_energy, grid_col * 2, 2, 0)
    row_term = jnp.broadcast_to(
        (row_occ[:, None] - vir_eff[None, :]).reshape(row_dev, 1), (row_dev, 128)
    )
    col_term = (col_occ[:, None] - vir_eff[None, :]).reshape(1, col_dev)

    own = load(t_store)
    pair = join(own, send(t_store, ACROSS_LO))
    beside = send(w_panels, OTHER_CORE)
    row_part, places = arranged(origin, block_place, row_term)
    near = join(after(pair, row_part, places, col_term, beside), send(pair, along_first(1)))
    far = join(after(send(pair, along_first(-1)), near), send(pair, along_first(2)))
    near_up = send(near, along_second(1))
    far_down = send(far, along_second(-1))
    far_up = send(far, along_second(1))
    near_down = send(after(near, far), along_second(-1))
    near_two = send(near_up, along_second(1))
    far_two = send(far_down, along_second(-1))

    across = send(after(w_panels, own), ACROSS_HI)
    so_far = begun(0, int(3 * 10**9), origin, (near, far), w_panels, beside, [])
    so_far = begun(1, int(3 * 10**9), origin, (near_up, far_down), w_panels, beside, so_far)
    so_far = begun(2, int(3 * 10**9), origin, (far_up, near_down), w_panels, beside, so_far, across)
    aslant = send(after(across, so_far[1]), OTHER_CORE)
    held, sums = begun(3, 12 * 10**9, origin, (near_two, far_two), w_panels, beside, so_far)
    return finished(origin, places, row_part, col_term, held, sums, across, aslant)


def solution(mesh):
    in_specs = (P(("row", "col"), None), P("row", "col"), P(), P(), P(), P())
    out_specs = P("row", "col")
    return jax.shard_map(
        per_device, mesh=mesh, in_specs=in_specs, out_specs=out_specs, check_vma=False
    )
```

```python
import functools

import jax
import jax.numpy as jnp
import numpy as np
from jax import lax
from jax.experimental import pallas as pl
from jax.experimental.pallas import tpu as pltpu
from jax.sharding import PartitionSpec as P

NVIR = 1024
BLK = 8
RING = 4
PIECE = 256
TILE = 256
STEP = 16


def move(target):
    pairs = []
    for src in range(128):
        row, col = divmod(src, 32)
        place = (row // 2) * 2 + col % 2, col // 2 % RING, col // 8, row % 2
        x, y, z, core = target(*place)
        x, y, z = x % RING, y % RING, z % RING
        pairs.append((src, (x // 2 * 2 + core) * 32 + z * 8 + y * 2 + x % 2))
    return pairs


def along_first(step):
    return move(lambda x, y, z, core: (x, y + step, z, core) if core == 0 else (x, y, z + step, core))


def along_second(step):
    return move(lambda x, y, z, core: (x, y, z + step, core) if core == 0 else (x, y + step, z, core))


ACROSS_LO = move(lambda x, y, z, core: (x ^ 1, y, z, core))
ACROSS_HI = move(lambda x, y, z, core: (x + 2, y, z, core))
OTHER_CORE = move(lambda x, y, z, core: (x, y, z, 1 - core))


def send(value, pairs):
    return lax.ppermute(value, ("row", "col"), pairs)


def after(value, *others):
    return lax.optimization_barrier((value, *others))[0]


def join_kernel(first, second, out):
    rows = first.shape[0]
    out[:rows, :] = first[...]
    out[rows:, :] = second[...]


def load_kernel(source, out, sem):
    copy = pltpu.make_async_copy(source, out, sem)
    copy.start()
    copy.wait()


def load(source):
    return pl.pallas_call(
        load_kernel,
        out_shape=jax.ShapeDtypeStruct(source.shape, source.dtype),
        in_specs=[pl.BlockSpec(memory_space=pl.ANY)],
        out_specs=pl.BlockSpec(memory_space=pltpu.VMEM),
        scratch_shapes=[pltpu.SemaphoreType.DMA],
        compiler_params=limits(1),
        cost_estimate=cost(0, 2**20),
    )(source)


def join(first, second):
    rows, cols = first.shape
    vmem = pl.BlockSpec(memory_space=pltpu.VMEM)
    return pl.pallas_call(
        join_kernel,
        out_shape=jax.ShapeDtypeStruct((2 * rows, cols), first.dtype),
        in_specs=[vmem, vmem],
        out_specs=vmem,
        compiler_params=limits(4),
        cost_estimate=cost(0, 8 * rows * cols),
    )(first, second)


def places_of(origin, block_place, group):
    shards = [origin[group * (STEP // BLK) + j] * BLK for j in range(STEP // BLK)]
    start = origin[32] * 256
    return [block_place[shards[j // BLK] + j % BLK] - start for j in range(STEP)]


def arrange(origin, block_place, row_term, row_part):
    def some(group, carry):
        at = [pl.multiple_of(place * BLK, BLK) for place in places_of(origin, block_place, group)]
        terms = [row_term[pl.ds(place, BLK), :] for place in at]
        for j, term in enumerate(terms):
            to = pl.multiple_of((group * STEP + j) * BLK, BLK)
            row_part[pl.ds(to, BLK), :] = term
        return carry

    lax.fori_loop(0, 256 // STEP, some, 0)


def list_places(origin, block_place, places):
    def some(group, carry):
        for j, place in enumerate(places_of(origin, block_place, group)):
            places[group * STEP + j] = place
        return carry

    lax.fori_loop(0, 256 // STEP, some, 0)


def stand(places, across, sums, mark):
    mark[...] = jnp.zeros_like(mark)


def begin(pair, origin, *refs):
    first, second, own, beside = refs[:4]
    held, sums = refs[-2:]
    grid_row = origin[32]
    rows = pl.ds(pair * 2 * PIECE, 2 * PIECE)
    held[pl.ds(pair * 2 * PIECE, PIECE), :] = first[...]
    held[pl.ds((pair * 2 + 1) * PIECE, PIECE), :] = second[...]

    def tile(i, carry):
        at = pl.ds(pl.multiple_of(i * TILE, TILE), TILE)
        total = None
        for chunk, panel in enumerate((own, beside)):
            depth = pl.ds(pl.multiple_of((grid_row ^ chunk) * 256, 256), 256)
            left = jnp.concatenate([first[:, depth], second[:, depth]])
            term = jnp.dot(left, panel[:, at], preferred_element_type=jnp.float32)
            total = term if total is None else total + term
        sums[rows, at] = total
        return carry

    lax.fori_loop(0, sums.shape[1] // TILE, tile, 0, unroll=4)


def finish(origin, places, row_part, col_term, held, sums, across, aslant, out, stage, sem):
    cols = col_term.shape[1]
    tiles, blocks = cols // TILE, 2 * PIECE // BLK
    depths = [pl.ds(pl.multiple_of((origin[32] ^ chunk) * 256, 256), 256) for chunk in (2, 3)]

    def gone(slot):
        pltpu.make_async_copy(
            stage.at[slot], out.at[pl.ds(0, 2 * PIECE), :], sem.at[slot]
        ).wait()

    def work(pair, carry):
        slot = pair % 2
        rows = pl.ds(pl.multiple_of(pair * 2 * PIECE, 2 * PIECE), 2 * PIECE)

        @pl.when(pair > 1)
        def _():
            gone(slot)

        def tile(i, carry):
            at = pl.ds(pl.multiple_of(i * TILE, TILE), TILE)
            total = sums[rows, at]
            for depth, panel in zip(depths, (across, aslant)):
                total += jnp.dot(held[rows, depth], panel[:, at], preferred_element_type=jnp.float32)
            left = row_part[rows, :]
            denominator = jnp.concatenate([left] * (TILE // 128), axis=1) + col_term[:, at]
            inverse = pltpu.reciprocal(denominator, approx=True)
            inverse = inverse * (2.0 - denominator * inverse)
            stage[slot, :, at] = total * inverse
            return carry

        lax.fori_loop(0, tiles, tile, 0, unroll=8)

        def put(i, carry):
            at = pl.multiple_of(i * BLK, BLK)
            to = pl.multiple_of(places[pair * blocks + i] * BLK, BLK)
            pltpu.make_async_copy(
                stage.at[slot, pl.ds(at, BLK), :], out.at[pl.ds(to, BLK), :], sem.at[slot]
            ).start()
            return carry

        lax.fori_loop(0, blocks, put, 0, unroll=64)
        return carry

    lax.fori_loop(0, 4, work, 0)
    gone(0)
    gone(1)


VMEM = pl.BlockSpec(memory_space=pltpu.VMEM)
SMEM = pl.BlockSpec(memory_space=pltpu.SMEM)


def limits(mebibytes):
    return pltpu.CompilerParams(vmem_limit_bytes=mebibytes * 2**20)


def cost(flops, moved):
    return pl.CostEstimate(flops=flops, bytes_accessed=moved, transcendentals=0)


def arranged(origin, block_place, row_term):
    return pl.pallas_call(
        arrange,
        out_shape=jax.ShapeDtypeStruct(row_term.shape, jnp.float32),
        in_specs=[SMEM, SMEM, VMEM],
        out_specs=VMEM,
        compiler_params=limits(4),
        cost_estimate=cost(3 * 10**9, 2**21),
    )(origin, block_place, row_term)


def listed(origin, block_place):
    return pl.pallas_call(
        list_places,
        out_shape=jax.ShapeDtypeStruct((256,), jnp.int32),
        in_specs=[SMEM, SMEM],
        out_specs=SMEM,
        compiler_params=limits(1),
        cost_estimate=cost(10**9, 2**20),
    )(origin, block_place)


def stood(places, across, sums):
    anywhere = pl.BlockSpec(memory_space=pl.ANY)
    return pl.pallas_call(
        stand,
        out_shape=jax.ShapeDtypeStruct((8, 128), jnp.float32),
        in_specs=[SMEM, anywhere, anywhere],
        out_specs=VMEM,
        compiler_params=limits(1),
        cost_estimate=cost(5 * 10**9, 2**12),
    )(places, across, sums)


def begun(pair, work, origin, pieces, own, beside, so_far, *awaited):
    cols, depth = own.shape[1], pieces[0].shape[1]
    shapes = [
        jax.ShapeDtypeStruct((8 * PIECE, depth), own.dtype),
        jax.ShapeDtypeStruct((8 * PIECE, cols), jnp.float32),
    ]
    operands = [origin, *pieces, own, beside, *so_far, *awaited]
    return pl.pallas_call(
        functools.partial(begin, pair),
        out_shape=shapes,
        in_specs=[SMEM]
        + [VMEM] * (len(operands) - 1 - len(awaited))
        + [pl.BlockSpec(memory_space=pl.ANY)] * len(awaited),
        out_specs=[VMEM, VMEM],
        input_output_aliases={5: 0, 6: 1} if so_far else {},
        compiler_params=limits(4),
        cost_estimate=cost(work, 2**21),
    )(*operands)


def finished(*operands):
    shape = operands[2].shape[0], operands[3].shape[1]
    return pl.pallas_call(
        finish,
        out_shape=jax.ShapeDtypeStruct(shape, jnp.float32),
        in_specs=[SMEM, SMEM] + [VMEM] * 6,
        out_specs=pl.BlockSpec(memory_space=pl.ANY),
        scratch_shapes=[
            pltpu.VMEM((2, 2 * PIECE, shape[1]), jnp.float32),
            pltpu.SemaphoreType.DMA((2,)),
        ],
        compiler_params=limits(12),
        cost_estimate=cost(1, 2**23),
    )(*operands)


NEAR = (0, 3)
FAR = (1, 2)
PIECES = [(NEAR, 0), (FAR, 0), (NEAR, 3), (FAR, 1), (FAR, 3), (NEAR, 1), (NEAR, 2), (FAR, 2)]


def per_device(t_store, w_panels, block_place, occ_energy, vir_energy, vir_order):
    grid_row = lax.axis_index("row")
    grid_col = lax.axis_index("col")
    core = grid_row % 2
    col_dev = w_panels.shape[1]
    row_dev = 2048

    first = np.array([step for steps, _ in PIECES for step in steps for _ in range(2)], np.int32)
    second = np.array([step for steps, step in PIECES for _ in range(4)], np.int32)
    other = np.array([0, 1] * 16, np.int32)
    y, z, lo = grid_col // 2 % RING, grid_col // 8, grid_col % 2
    at_first = (jnp.where(core == 0, y, z) + first) % RING
    at_second = (jnp.where(core == 0, z, y) + second) % RING
    at_y = jnp.where(core == 0, at_first, at_second)
    at_z = jnp.where(core == 0, at_second, at_first)
    origin = grid_row * 32 + at_z * 8 + at_y * 2 + (lo ^ other)
    origin = jnp.concatenate([origin, grid_row[None]]).astype(jnp.int32)

    indices = jnp.arange(NVIR, dtype=jnp.int32)
    vir_eff = jnp.sum(
        jnp.where(vir_order[:, None] == indices[None, :], vir_energy[None, :], 0.0), axis=1
    )
    row_occ = lax.dynamic_slice_in_dim(occ_energy, grid_row * 2, 2, 0)
    col_occ = lax.dynamic_slice_in_dim(occ_energy, grid_col * 2, 2, 0)
    row_term = jnp.broadcast_to(
        (row_occ[:, None] - vir_eff[None, :]).reshape(row_dev, 1), (row_dev, 128)
    )
    col_term = (col_occ[:, None] - vir_eff[None, :]).reshape(1, col_dev)

    own = load(t_store)
    fetched = send(t_store, ACROSS_LO)
    pair = join(after(own, row_term, col_term), fetched)
    row_part = arranged(origin, block_place, row_term)
    beside = send(after(w_panels, pair), OTHER_CORE)
    near = join(after(pair, beside), send(pair, along_first(1)))
    far = join(after(send(pair, along_first(-1)), near), send(pair, along_first(2)))
    near_up = send(near, along_second(1))
    far_down = send(far, along_second(-1))
    far_up = send(far, along_second(1))
    near_down = send(after(near, far), along_second(-1))
    near_two = send(near_up, along_second(1))
    far_two = send(far_down, along_second(-1))

    across = send(after(w_panels, fetched), ACROSS_HI)
    so_far = begun(0, 3 * 10**9, origin, (near, far), w_panels, beside, [])
    so_far = begun(1, 3 * 10**9, origin, (near_up, far_down), w_panels, beside, so_far)
    so_far = begun(2, 1 * 10**9, origin, (far_up, near_down), w_panels, beside, so_far, row_part)
    places = listed(origin, block_place)
    mark = stood(places, across, so_far[1])
    aslant = send(after(across, mark), OTHER_CORE)
    held, sums = begun(3, 12 * 10**9, origin, (near_two, far_two), w_panels, beside, so_far, mark)
    return finished(origin, places, row_part, col_term, held, sums, across, aslant)


def solution(mesh):
    in_specs = (P(("row", "col"), None), P("row", "col"), P(), P(), P(), P())
    out_specs = P("row", "col")
    return jax.shard_map(
        per_device, mesh=mesh, in_specs=in_specs, out_specs=out_specs, check_vma=False
    )
```

```python
import functools

import jax
import jax.numpy as jnp
import numpy as np
from jax import lax
from jax.experimental import pallas as pl
from jax.experimental.pallas import tpu as pltpu
from jax.sharding import PartitionSpec as P

NVIR = 1024
BLK = 8
RING = 4
PIECE = 256
TILE = 256
STEP = 16


def move(target):
    pairs = []
    for src in range(128):
        row, col = divmod(src, 32)
        place = (row // 2) * 2 + col % 2, col // 2 % RING, col // 8, row % 2
        x, y, z, core = target(*place)
        x, y, z = x % RING, y % RING, z % RING
        pairs.append((src, (x // 2 * 2 + core) * 32 + z * 8 + y * 2 + x % 2))
    return pairs


def along_first(step):
    return move(lambda x, y, z, core: (x, y + step, z, core) if core == 0 else (x, y, z + step, core))


def along_second(step):
    return move(lambda x, y, z, core: (x, y, z + step, core) if core == 0 else (x, y + step, z, core))


ACROSS_LO = move(lambda x, y, z, core: (x ^ 1, y, z, core))
ACROSS_HI = move(lambda x, y, z, core: (x + 2, y, z, core))
OTHER_CORE = move(lambda x, y, z, core: (x, y, z, 1 - core))


def send(value, pairs):
    return lax.ppermute(value, ("row", "col"), pairs)


def after(value, *others):
    return lax.optimization_barrier((value, *others))[0]


def join_kernel(first, second, out):
    rows = first.shape[0]
    out[:rows, :] = first[...]
    out[rows:, :] = second[...]


def load_kernel(source, out, sem):
    copy = pltpu.make_async_copy(source, out, sem)
    copy.start()
    copy.wait()


def load(source):
    return pl.pallas_call(
        load_kernel,
        out_shape=jax.ShapeDtypeStruct(source.shape, source.dtype),
        in_specs=[pl.BlockSpec(memory_space=pl.ANY)],
        out_specs=pl.BlockSpec(memory_space=pltpu.VMEM),
        scratch_shapes=[pltpu.SemaphoreType.DMA],
        compiler_params=limits(1),
        cost_estimate=cost(0, 2**20),
    )(source)


def join(first, second):
    rows, cols = first.shape
    vmem = pl.BlockSpec(memory_space=pltpu.VMEM)
    return pl.pallas_call(
        join_kernel,
        out_shape=jax.ShapeDtypeStruct((2 * rows, cols), first.dtype),
        in_specs=[vmem, vmem],
        out_specs=vmem,
        compiler_params=limits(4),
        cost_estimate=cost(0, 8 * rows * cols),
    )(first, second)


def places_of(origin, block_place, group):
    shards = [origin[group * (STEP // BLK) + j] * BLK for j in range(STEP // BLK)]
    start = origin[32] * 256
    return [block_place[shards[j // BLK] + j % BLK] - start for j in range(STEP)]


def arrange(origin, block_place, row_term, row_part):
    def some(group, carry):
        at = [pl.multiple_of(place * BLK, BLK) for place in places_of(origin, block_place, group)]
        terms = [row_term[pl.ds(place, BLK), :] for place in at]
        for j, term in enumerate(terms):
            to = pl.multiple_of((group * STEP + j) * BLK, BLK)
            row_part[pl.ds(to, BLK), :] = term
        return carry

    lax.fori_loop(0, 256 // STEP, some, 0)


def list_places(origin, block_place, places):
    def some(group, carry):
        for j, place in enumerate(places_of(origin, block_place, group)):
            places[group * STEP + j] = place
        return carry

    lax.fori_loop(0, 256 // STEP, some, 0)


def stand(across, sums, mark):
    mark[...] = jnp.zeros_like(mark)


def begin(pair, origin, *refs):
    first, second, own, beside = refs[:4]
    held, sums = refs[-2:]
    grid_row = origin[32]
    rows = pl.ds(pair * 2 * PIECE, 2 * PIECE)
    held[pl.ds(pair * 2 * PIECE, PIECE), :] = first[...]
    held[pl.ds((pair * 2 + 1) * PIECE, PIECE), :] = second[...]

    def tile(i, carry):
        at = pl.ds(pl.multiple_of(i * TILE, TILE), TILE)
        total = None
        for chunk, panel in enumerate((own, beside)):
            depth = pl.ds(pl.multiple_of((grid_row ^ chunk) * 256, 256), 256)
            left = jnp.concatenate([first[:, depth], second[:, depth]])
            term = jnp.dot(left, panel[:, at], preferred_element_type=jnp.float32)
            total = term if total is None else total + term
        sums[rows, at] = total
        return carry

    lax.fori_loop(0, sums.shape[1] // TILE, tile, 0, unroll=4)


def finish(origin, places, row_part, col_term, held, sums, across, aslant, out, stage, sem):
    cols = col_term.shape[1]
    tiles, blocks = cols // TILE, 2 * PIECE // BLK
    depths = [pl.ds(pl.multiple_of((origin[32] ^ chunk) * 256, 256), 256) for chunk in (2, 3)]

    def gone(slot):
        pltpu.make_async_copy(
            stage.at[slot], out.at[pl.ds(0, 2 * PIECE), :], sem.at[slot]
        ).wait()

    def work(pair, carry):
        slot = pair % 2
        rows = pl.ds(pl.multiple_of(pair * 2 * PIECE, 2 * PIECE), 2 * PIECE)

        @pl.when(pair > 1)
        def _():
            gone(slot)

        def tile(i, carry):
            at = pl.ds(pl.multiple_of(i * TILE, TILE), TILE)
            total = sums[rows, at]
            for depth, panel in zip(depths, (across, aslant)):
                total += jnp.dot(held[rows, depth], panel[:, at], preferred_element_type=jnp.float32)
            left = row_part[rows, :]
            denominator = jnp.concatenate([left] * (TILE // 128), axis=1) + col_term[:, at]
            inverse = pltpu.reciprocal(denominator, approx=True)
            inverse = inverse * (2.0 - denominator * inverse)
            stage[slot, :, at] = total * inverse
            return carry

        lax.fori_loop(0, tiles, tile, 0, unroll=8)

        def put(i, carry):
            at = pl.multiple_of(i * BLK, BLK)
            to = pl.multiple_of(places[pair * blocks + i] * BLK, BLK)
            pltpu.make_async_copy(
                stage.at[slot, pl.ds(at, BLK), :], out.at[pl.ds(to, BLK), :], sem.at[slot]
            ).start()
            return carry

        lax.fori_loop(0, blocks, put, 0, unroll=64)
        return carry

    lax.fori_loop(0, 4, work, 0)
    gone(0)
    gone(1)


VMEM = pl.BlockSpec(memory_space=pltpu.VMEM)
SMEM = pl.BlockSpec(memory_space=pltpu.SMEM)


def limits(mebibytes):
    return pltpu.CompilerParams(vmem_limit_bytes=mebibytes * 2**20)


def cost(flops, moved):
    return pl.CostEstimate(flops=flops, bytes_accessed=moved, transcendentals=0)


def arranged(origin, block_place, row_term):
    return pl.pallas_call(
        arrange,
        out_shape=jax.ShapeDtypeStruct(row_term.shape, jnp.float32),
        in_specs=[SMEM, SMEM, VMEM],
        out_specs=VMEM,
        compiler_params=limits(4),
        cost_estimate=cost(3 * 10**9, 2**21),
    )(origin, block_place, row_term)


def listed(origin, block_place):
    return pl.pallas_call(
        list_places,
        out_shape=jax.ShapeDtypeStruct((256,), jnp.int32),
        in_specs=[SMEM, SMEM],
        out_specs=SMEM,
        compiler_params=limits(1),
        cost_estimate=cost(10**9, 2**20),
    )(origin, block_place)


def stood(across, sums):
    anywhere = pl.BlockSpec(memory_space=pl.ANY)
    return pl.pallas_call(
        stand,
        out_shape=jax.ShapeDtypeStruct((8, 128), jnp.float32),
        in_specs=[anywhere, anywhere],
        out_specs=VMEM,
        compiler_params=limits(1),
        cost_estimate=cost(5 * 10**9, 2**12),
    )(across, sums)


def begun(pair, work, origin, pieces, own, beside, so_far, *awaited):
    cols, depth = own.shape[1], pieces[0].shape[1]
    shapes = [
        jax.ShapeDtypeStruct((8 * PIECE, depth), own.dtype),
        jax.ShapeDtypeStruct((8 * PIECE, cols), jnp.float32),
    ]
    operands = [origin, *pieces, own, beside, *so_far, *awaited]
    return pl.pallas_call(
        functools.partial(begin, pair),
        out_shape=shapes,
        in_specs=[SMEM]
        + [VMEM] * (len(operands) - 1 - len(awaited))
        + [SMEM if x.dtype == jnp.int32 else pl.BlockSpec(memory_space=pl.ANY) for x in awaited],
        out_specs=[VMEM, VMEM],
        input_output_aliases={5: 0, 6: 1} if so_far else {},
        compiler_params=limits(4),
        cost_estimate=cost(work, 2**21),
    )(*operands)


def finished(*operands):
    shape = operands[2].shape[0], operands[3].shape[1]
    return pl.pallas_call(
        finish,
        out_shape=jax.ShapeDtypeStruct(shape, jnp.float32),
        in_specs=[SMEM, SMEM] + [VMEM] * 6,
        out_specs=pl.BlockSpec(memory_space=pl.ANY),
        scratch_shapes=[
            pltpu.VMEM((2, 2 * PIECE, shape[1]), jnp.float32),
            pltpu.SemaphoreType.DMA((2,)),
        ],
        compiler_params=limits(12),
        cost_estimate=cost(1, 2**23),
    )(*operands)


NEAR = (0, 3)
FAR = (1, 2)
PIECES = [(NEAR, 0), (FAR, 0), (NEAR, 3), (FAR, 1), (FAR, 3), (NEAR, 1), (NEAR, 2), (FAR, 2)]


def per_device(t_store, w_panels, block_place, occ_energy, vir_energy, vir_order):
    grid_row = lax.axis_index("row")
    grid_col = lax.axis_index("col")
    core = grid_row % 2
    col_dev = w_panels.shape[1]
    row_dev = 2048

    first = np.array([step for steps, _ in PIECES for step in steps for _ in range(2)], np.int32)
    second = np.array([step for steps, step in PIECES for _ in range(4)], np.int32)
    other = np.array([0, 1] * 16, np.int32)
    y, z, lo = grid_col // 2 % RING, grid_col // 8, grid_col % 2
    at_first = (jnp.where(core == 0, y, z) + first) % RING
    at_second = (jnp.where(core == 0, z, y) + second) % RING
    at_y = jnp.where(core == 0, at_first, at_second)
    at_z = jnp.where(core == 0, at_second, at_first)
    origin = grid_row * 32 + at_z * 8 + at_y * 2 + (lo ^ other)
    origin = jnp.concatenate([origin, grid_row[None]]).astype(jnp.int32)

    indices = jnp.arange(NVIR, dtype=jnp.int32)
    vir_eff = jnp.sum(
        jnp.where(vir_order[:, None] == indices[None, :], vir_energy[None, :], 0.0), axis=1
    )
    row_occ = lax.dynamic_slice_in_dim(occ_energy, grid_row * 2, 2, 0)
    col_occ = lax.dynamic_slice_in_dim(occ_energy, grid_col * 2, 2, 0)
    row_term = jnp.broadcast_to(
        (row_occ[:, None] - vir_eff[None, :]).reshape(row_dev, 1), (row_dev, 128)
    )
    col_term = (col_occ[:, None] - vir_eff[None, :]).reshape(1, col_dev)

    own = load(t_store)
    fetched = send(t_store, ACROSS_LO)
    pair = join(after(own, row_term, col_term), fetched)
    row_part = arranged(origin, block_place, row_term)
    beside = send(after(w_panels, pair), OTHER_CORE)
    near = join(after(pair, beside), send(pair, along_first(1)))
    far = join(after(send(pair, along_first(-1)), near), send(pair, along_first(2)))
    near_up = send(near, along_second(1))
    far_down = send(far, along_second(-1))
    far_up = send(far, along_second(1))
    near_down = send(after(near, far), along_second(-1))
    near_two = send(near_up, along_second(1))
    far_two = send(far_down, along_second(-1))

    across = send(after(w_panels, fetched), ACROSS_HI)
    places = listed(origin, block_place)
    so_far = begun(0, 3 * 10**9, origin, (near, far), w_panels, beside, [])
    so_far = begun(1, 3 * 10**9, origin, (near_up, far_down), w_panels, beside, so_far, places)
    so_far = begun(2, 1 * 10**9, origin, (far_up, near_down), w_panels, beside, so_far, row_part)
    mark = stood(across, so_far[1])
    aslant = send(after(across, mark), OTHER_CORE)
    held, sums = begun(3, 12 * 10**9, origin, (near_two, far_two), w_panels, beside, so_far, mark)
    return finished(origin, places, row_part, col_term, held, sums, across, aslant)


def solution(mesh):
    in_specs = (P(("row", "col"), None), P("row", "col"), P(), P(), P(), P())
    out_specs = P("row", "col")
    return jax.shard_map(
        per_device, mesh=mesh, in_specs=in_specs, out_specs=out_specs, check_vma=False
    )
```

```python
import functools

import jax
import jax.numpy as jnp
import numpy as np
from jax import lax
from jax.experimental import pallas as pl
from jax.experimental.pallas import tpu as pltpu
from jax.sharding import PartitionSpec as P

NVIR = 1024
BLK = 8
RING = 4
PIECE = 256
TILE = 256
STEP = 16


def move(target):
    pairs = []
    for src in range(128):
        row, col = divmod(src, 32)
        place = (row // 2) * 2 + col % 2, col // 2 % RING, col // 8, row % 2
        x, y, z, core = target(*place)
        x, y, z = x % RING, y % RING, z % RING
        pairs.append((src, (x // 2 * 2 + core) * 32 + z * 8 + y * 2 + x % 2))
    return pairs


def along_first(step):
    return move(lambda x, y, z, core: (x, y + step, z, core) if core == 0 else (x, y, z + step, core))


def along_second(step):
    return move(lambda x, y, z, core: (x, y, z + step, core) if core == 0 else (x, y + step, z, core))


ACROSS_LO = move(lambda x, y, z, core: (x ^ 1, y, z, core))
ACROSS_HI = move(lambda x, y, z, core: (x + 2, y, z, core))
OTHER_CORE = move(lambda x, y, z, core: (x, y, z, 1 - core))


def send(value, pairs):
    return lax.ppermute(value, ("row", "col"), pairs)


def after(value, *others):
    return lax.optimization_barrier((value, *others))[0]


def join_kernel(first, second, out):
    rows = first.shape[0]
    out[:rows, :] = first[...]
    out[rows:, :] = second[...]


def load_kernel(source, out, sem):
    copy = pltpu.make_async_copy(source, out, sem)
    copy.start()
    copy.wait()


def load(source):
    return pl.pallas_call(
        load_kernel,
        out_shape=jax.ShapeDtypeStruct(source.shape, source.dtype),
        in_specs=[pl.BlockSpec(memory_space=pl.ANY)],
        out_specs=pl.BlockSpec(memory_space=pltpu.VMEM),
        scratch_shapes=[pltpu.SemaphoreType.DMA],
        compiler_params=limits(1),
        cost_estimate=cost(0, 2**20),
    )(source)


def join(first, second):
    rows, cols = first.shape
    vmem = pl.BlockSpec(memory_space=pltpu.VMEM)
    return pl.pallas_call(
        join_kernel,
        out_shape=jax.ShapeDtypeStruct((2 * rows, cols), first.dtype),
        in_specs=[vmem, vmem],
        out_specs=vmem,
        compiler_params=limits(4),
        cost_estimate=cost(0, 8 * rows * cols),
    )(first, second)


def places_of(origin, block_place, group):
    shards = [origin[group * (STEP // BLK) + j] * BLK for j in range(STEP // BLK)]
    start = origin[32] * 256
    return [block_place[shards[j // BLK] + j % BLK] - start for j in range(STEP)]


def arrange(origin, block_place, row_term, row_part):
    def some(group, carry):
        at = [pl.multiple_of(place * BLK, BLK) for place in places_of(origin, block_place, group)]
        terms = [row_term[pl.ds(place, BLK), :] for place in at]
        for j, term in enumerate(terms):
            to = pl.multiple_of((group * STEP + j) * BLK, BLK)
            row_part[pl.ds(to, BLK), :] = term
        return carry

    lax.fori_loop(0, 256 // STEP, some, 0)


def list_places(origin, block_place, places):
    def some(group, carry):
        for j, place in enumerate(places_of(origin, block_place, group)):
            places[group * STEP + j] = place
        return carry

    lax.fori_loop(0, 256 // STEP, some, 0)


def stand(across, sums, mark):
    mark[...] = jnp.zeros_like(mark)


def begin(pair, origin, *refs):
    first, second, own, beside = refs[:4]
    held, sums = refs[-2:]
    grid_row = origin[32]
    rows = pl.ds(pair * 2 * PIECE, 2 * PIECE)
    held[pl.ds(pair * 2 * PIECE, PIECE), :] = first[...]
    held[pl.ds((pair * 2 + 1) * PIECE, PIECE), :] = second[...]

    def tile(i, carry):
        at = pl.ds(pl.multiple_of(i * TILE, TILE), TILE)
        total = None
        for chunk, panel in enumerate((own, beside)):
            depth = pl.ds(pl.multiple_of((grid_row ^ chunk) * 256, 256), 256)
            left = jnp.concatenate([first[:, depth], second[:, depth]])
            term = jnp.dot(left, panel[:, at], preferred_element_type=jnp.float32)
            total = term if total is None else total + term
        sums[rows, at] = total
        return carry

    lax.fori_loop(0, sums.shape[1] // TILE, tile, 0, unroll=8)


def finish(origin, places, row_part, col_term, held, sums, across, aslant, out, stage, sem):
    cols = col_term.shape[1]
    tiles, blocks = cols // TILE, 2 * PIECE // BLK
    depths = [pl.ds(pl.multiple_of((origin[32] ^ chunk) * 256, 256), 256) for chunk in (2, 3)]

    def gone(slot):
        pltpu.make_async_copy(
            stage.at[slot], out.at[pl.ds(0, 2 * PIECE), :], sem.at[slot]
        ).wait()

    def work(pair, carry):
        slot = pair % 2
        rows = pl.ds(pl.multiple_of(pair * 2 * PIECE, 2 * PIECE), 2 * PIECE)

        @pl.when(pair > 1)
        def _():
            gone(slot)

        def tile(i, carry):
            at = pl.ds(pl.multiple_of(i * TILE, TILE), TILE)
            total = sums[rows, at]
            for depth, panel in zip(depths, (across, aslant)):
                total += jnp.dot(held[rows, depth], panel[:, at], preferred_element_type=jnp.float32)
            left = row_part[rows, :]
            denominator = jnp.concatenate([left] * (TILE // 128), axis=1) + col_term[:, at]
            inverse = pltpu.reciprocal(denominator, approx=True)
            inverse = inverse * (2.0 - denominator * inverse)
            stage[slot, :, at] = total * inverse
            return carry

        lax.fori_loop(0, tiles, tile, 0, unroll=8)

        def put(i, carry):
            at = pl.multiple_of(i * BLK, BLK)
            to = pl.multiple_of(places[pair * blocks + i] * BLK, BLK)
            pltpu.make_async_copy(
                stage.at[slot, pl.ds(at, BLK), :], out.at[pl.ds(to, BLK), :], sem.at[slot]
            ).start()
            return carry

        lax.fori_loop(0, blocks, put, 0, unroll=64)
        return carry

    lax.fori_loop(0, 4, work, 0)
    gone(0)
    gone(1)


VMEM = pl.BlockSpec(memory_space=pltpu.VMEM)
SMEM = pl.BlockSpec(memory_space=pltpu.SMEM)


def limits(mebibytes):
    return pltpu.CompilerParams(vmem_limit_bytes=mebibytes * 2**20)


def cost(flops, moved):
    return pl.CostEstimate(flops=flops, bytes_accessed=moved, transcendentals=0)


def arranged(origin, block_place, row_term):
    return pl.pallas_call(
        arrange,
        out_shape=jax.ShapeDtypeStruct(row_term.shape, jnp.float32),
        in_specs=[SMEM, SMEM, VMEM],
        out_specs=VMEM,
        compiler_params=limits(4),
        cost_estimate=cost(3 * 10**9, 2**21),
    )(origin, block_place, row_term)


def listed(origin, block_place):
    return pl.pallas_call(
        list_places,
        out_shape=jax.ShapeDtypeStruct((256,), jnp.int32),
        in_specs=[SMEM, SMEM],
        out_specs=SMEM,
        compiler_params=limits(1),
        cost_estimate=cost(10**9, 2**20),
    )(origin, block_place)


def stood(across, sums):
    anywhere = pl.BlockSpec(memory_space=pl.ANY)
    return pl.pallas_call(
        stand,
        out_shape=jax.ShapeDtypeStruct((8, 128), jnp.float32),
        in_specs=[anywhere, anywhere],
        out_specs=VMEM,
        compiler_params=limits(1),
        cost_estimate=cost(5 * 10**9, 2**12),
    )(across, sums)


def begun(pair, work, origin, pieces, own, beside, so_far, *awaited):
    cols, depth = own.shape[1], pieces[0].shape[1]
    shapes = [
        jax.ShapeDtypeStruct((8 * PIECE, depth), own.dtype),
        jax.ShapeDtypeStruct((8 * PIECE, cols), jnp.float32),
    ]
    operands = [origin, *pieces, own, beside, *so_far, *awaited]
    return pl.pallas_call(
        functools.partial(begin, pair),
        out_shape=shapes,
        in_specs=[SMEM]
        + [VMEM] * (len(operands) - 1 - len(awaited))
        + [SMEM if x.dtype == jnp.int32 else pl.BlockSpec(memory_space=pl.ANY) for x in awaited],
        out_specs=[VMEM, VMEM],
        input_output_aliases={5: 0, 6: 1} if so_far else {},
        compiler_params=limits(4),
        cost_estimate=cost(work, 2**21),
    )(*operands)


def finished(*operands):
    shape = operands[2].shape[0], operands[3].shape[1]
    return pl.pallas_call(
        finish,
        out_shape=jax.ShapeDtypeStruct(shape, jnp.float32),
        in_specs=[SMEM, SMEM] + [VMEM] * 6,
        out_specs=pl.BlockSpec(memory_space=pl.ANY),
        scratch_shapes=[
            pltpu.VMEM((2, 2 * PIECE, shape[1]), jnp.float32),
            pltpu.SemaphoreType.DMA((2,)),
        ],
        compiler_params=limits(12),
        cost_estimate=cost(1, 2**23),
    )(*operands)


NEAR = (0, 3)
FAR = (1, 2)
PIECES = [(NEAR, 0), (FAR, 0), (NEAR, 3), (FAR, 1), (FAR, 3), (NEAR, 1), (NEAR, 2), (FAR, 2)]


def per_device(t_store, w_panels, block_place, occ_energy, vir_energy, vir_order):
    grid_row = lax.axis_index("row")
    grid_col = lax.axis_index("col")
    core = grid_row % 2
    col_dev = w_panels.shape[1]
    row_dev = 2048

    first = np.array([step for steps, _ in PIECES for step in steps for _ in range(2)], np.int32)
    second = np.array([step for steps, step in PIECES for _ in range(4)], np.int32)
    other = np.array([0, 1] * 16, np.int32)
    y, z, lo = grid_col // 2 % RING, grid_col // 8, grid_col % 2
    at_first = (jnp.where(core == 0, y, z) + first) % RING
    at_second = (jnp.where(core == 0, z, y) + second) % RING
    at_y = jnp.where(core == 0, at_first, at_second)
    at_z = jnp.where(core == 0, at_second, at_first)
    origin = grid_row * 32 + at_z * 8 + at_y * 2 + (lo ^ other)
    origin = jnp.concatenate([origin, grid_row[None]]).astype(jnp.int32)

    indices = jnp.arange(NVIR, dtype=jnp.int32)
    vir_eff = jnp.sum(
        jnp.where(vir_order[:, None] == indices[None, :], vir_energy[None, :], 0.0), axis=1
    )
    row_occ = lax.dynamic_slice_in_dim(occ_energy, grid_row * 2, 2, 0)
    col_occ = lax.dynamic_slice_in_dim(occ_energy, grid_col * 2, 2, 0)
    row_term = jnp.broadcast_to(
        (row_occ[:, None] - vir_eff[None, :]).reshape(row_dev, 1), (row_dev, 128)
    )
    col_term = (col_occ[:, None] - vir_eff[None, :]).reshape(1, col_dev)

    own = load(t_store)
    fetched = send(t_store, ACROSS_LO)
    pair = join(after(own, row_term, col_term), fetched)
    row_part = arranged(origin, block_place, row_term)
    beside = send(after(w_panels, pair), OTHER_CORE)
    near = join(after(pair, beside), send(pair, along_first(1)))
    far = join(after(send(pair, along_first(-1)), near), send(pair, along_first(2)))
    near_up = send(near, along_second(1))
    far_down = send(far, along_second(-1))
    far_up = send(far, along_second(1))
    near_down = send(after(near, far), along_second(-1))
    near_two = send(near_up, along_second(1))
    far_two = send(far_down, along_second(-1))

    across = send(after(w_panels, fetched), ACROSS_HI)
    places = listed(origin, block_place)
    so_far = begun(0, 3 * 10**9, origin, (near, far), w_panels, beside, [])
    so_far = begun(1, 3 * 10**9, origin, (near_up, far_down), w_panels, beside, so_far, places)
    so_far = begun(2, 1 * 10**9, origin, (far_up, near_down), w_panels, beside, so_far, row_part)
    mark = stood(across, so_far[1])
    aslant = send(after(across, mark), OTHER_CORE)
    held, sums = begun(3, 12 * 10**9, origin, (near_two, far_two), w_panels, beside, so_far, mark)
    return finished(origin, places, row_part, col_term, held, sums, across, aslant)


def solution(mesh):
    in_specs = (P(("row", "col"), None), P("row", "col"), P(), P(), P(), P())
    out_specs = P("row", "col")
    return jax.shard_map(
        per_device, mesh=mesh, in_specs=in_specs, out_specs=out_specs, check_vma=False
    )
```
